32 devices in a mesh: region: 4 (over z), rows: 8 (over y, x, core).
Axes of the slice: x: 2, y: 2, z: 4, core: 2. Of those that a mesh axis runs over, the one named last changes fastest.
Arguments:
- ensemble_state: float32 [65536, 256], P(('region', 'rows')), may hold values from -16 to 16
- obs_values: float32 [4, 1024], replicated, may hold values from -16 to 16
- obs_error: float32 [4, 1024], replicated, may hold values from 0.1 to 2
- batch_owner: int32 [4], replicated, may hold values from 0 to 3
- readers: int32 [4, 3], replicated, may hold values from 0 to 3
- obs_order: int32 [4, 1024], replicated, may hold values from 0 to 1023, each once within a row
- obs_rows: int32 [4, 1024], replicated, may hold values from 0 to 2047
- loc_taper: float32 [4, 4, 1024], replicated, may hold values from 0.02 to 0.3
Outputs:
- analysis: float32 [65536, 256], P(('region', 'rows'))
The draws below stay inside these ranges and needn't reach their ends.
Inputs may be any that keep to these rules, and one draw needn't show every extreme that they name: Each row of obs_order holds every observation number once. `readers`: regions that read a batch besides its owner region; repeats allowed.
All inputs are finite; a program needn't handle non-finite values.
Results may differ from the reference program's by a relative error of at most 0.0024.
Values may be sent and summed in bfloat16 or wider, within the bound.
A program may use at most 64 MiB of HBM per device.

```python
import math
import jax
import jax.numpy as jnp
from jax import lax

MEMBERS = 256
OBS = 1024
BATCHES = 4
READERS = 3
ROWS_DEV = 2048
REGIONS = 4
GROUP = 8
SLOTS = 128
STATE_ROWS = 65536


def draw_ensemble_state(key, part):
    key_centre, key_spread, key_noise = jax.random.split(key, 3)
    centre = jax.random.uniform(key_centre, (STATE_ROWS, 1), jnp.float32, -8.0, 8.0)
    spread = jnp.exp(jax.random.uniform(key_spread, (STATE_ROWS, 1), jnp.float32, math.log(0.2), math.log(2.0)))
    noise_part = jnp.clip(jax.random.normal(key_noise, (STATE_ROWS, MEMBERS), jnp.float32), -3.5, 3.5)
    return centre + spread * noise_part


def plant(array, key, low, high):
    index_at = [jax.random.randint(jax.random.fold_in(key, axis), (), 0, length) for axis, length in enumerate(array.shape)]
    main_axis = array.shape.index(max(array.shape))
    beside = index_at[:main_axis] + [(index_at[main_axis] + 1) % array.shape[main_axis]] + index_at[main_axis + 1:]
    return array.at[tuple(index_at)].set(low).at[tuple(beside)].set(high)


def centred(own_key, dims, scale, bound, kind=jnp.bfloat16):
    result = jax.random.normal(own_key, dims, jnp.float32) * scale
    return jnp.minimum(jnp.maximum(result, -bound), bound).astype(kind)


def setup_inputs(seed: int = 0) -> dict:
    streams_of = jax.random.split(jax.random.key(seed), 9)
    ensemble_state = draw_ensemble_state(jax.random.fold_in(streams_of[8], 71), 0)
    obs_values = centred(streams_of[1], (BATCHES, OBS), 3.0, 16.0, jnp.float32)
    obs_error = jnp.clip(jnp.exp(jax.random.uniform(streams_of[2], (BATCHES, OBS), jnp.float32, math.log(0.1), math.log(2.0))), 0.1, 2.0)
    batch_owner = plant(jax.random.randint(streams_of[3], (BATCHES,), 0, REGIONS), jax.random.fold_in(streams_of[3], 1), 0, REGIONS - 1).astype(jnp.int32)
    readers = plant(jax.random.randint(streams_of[4], (BATCHES, READERS), 0, REGIONS), jax.random.fold_in(streams_of[4], 1), 0, REGIONS - 1).astype(jnp.int32)
    obs_order = jax.vmap(lambda own: jax.random.permutation(own, OBS))(jax.random.split(streams_of[5], BATCHES)).reshape((BATCHES, OBS)).astype(jnp.int32)
    obs_rows = plant(jax.random.randint(streams_of[6], (BATCHES, OBS), 0, ROWS_DEV), jax.random.fold_in(streams_of[6], 1), 0, ROWS_DEV - 1).astype(jnp.int32)
    loc_taper = jnp.clip(jnp.exp(jax.random.uniform(streams_of[7], (BATCHES, REGIONS, OBS), jnp.float32, math.log(0.02), math.log(0.3))), 0.02, 0.3)
    return dict(ensemble_state=ensemble_state, obs_values=obs_values, obs_error=obs_error, batch_owner=batch_owner, readers=readers, obs_order=obs_order, obs_rows=obs_rows, loc_taper=loc_taper)


def adjust(prior_ens, values, errors):
    members = prior_ens.shape[1]
    prior_mean = lax.optimization_barrier(jnp.mean(prior_ens, axis=1, keepdims=True))
    anomalies = prior_ens - prior_mean
    variance = lax.optimization_barrier(jnp.sum(anomalies * anomalies, axis=1, keepdims=True)) / (members - 1) + 1e-05
    errors = errors[:, None]
    values = values[:, None]
    post_var = variance * errors / (variance + errors)
    mean_shift = post_var * (prior_mean / variance + values / errors) - prior_mean
    shrink = jnp.sqrt(errors / (variance + errors))
    obs_incr = (mean_shift + (shrink - 1.0) * anomalies).astype(jnp.bfloat16)
    scaled = (anomalies / ((members - 1) * variance)).astype(jnp.bfloat16)
    return (scaled, obs_incr)

def update_block(block_x, scaled, obs_incr, weights):
    centre = lax.optimization_barrier(jnp.mean(block_x, axis=1, keepdims=True))
    state_anom = (block_x - centre).astype(jnp.bfloat16)
    linked = lax.dot_general(state_anom, scaled, (((1,), (1,)), ((), ())), preferred_element_type=jnp.float32)
    coupling = (linked * weights[None, :]).astype(jnp.bfloat16)
    return block_x + jnp.dot(coupling, obs_incr, preferred_element_type=jnp.float32)

def reference(ensemble_state, obs_values, obs_error, batch_owner, readers, obs_order, obs_rows, loc_taper):
    members = ensemble_state.shape[1]
    blocks = ensemble_state.reshape(REGIONS * GROUP, ROWS_DEV, members)
    block_region = (jnp.arange(REGIONS * GROUP) // GROUP).astype(jnp.int32)
    slot_column = (jnp.arange(OBS) // SLOTS).astype(jnp.int32)
    region_ids = jnp.arange(REGIONS).astype(jnp.int32)
    for batch_idx in range(BATCHES):
        source = (batch_owner[batch_idx] * GROUP + slot_column).astype(jnp.int32)
        picked = blocks[source, obs_rows[batch_idx]]
        prior_ens = jnp.zeros((OBS, members), jnp.float32).at[obs_order[batch_idx]].set(picked)
        scaled, obs_incr = adjust(prior_ens, obs_values[batch_idx], obs_error[batch_idx])
        reads_mask = jnp.logical_or(region_ids == batch_owner[batch_idx], jnp.any(readers[batch_idx][None, :] == region_ids[:, None], axis=1))
        tapers = loc_taper[batch_idx]

        def advance(entry_pair, scaled=scaled, obs_incr=obs_incr, reads_mask=reads_mask, tapers=tapers):
            block_x, region = entry_pair
            return lax.cond(reads_mask[region], lambda rows_x: update_block(rows_x, scaled, obs_incr, tapers[region]), lambda rows_x: rows_x, block_x)
        blocks = lax.map(advance, (blocks, block_region))
    return blocks.reshape(STATE_ROWS, members)
```

```python
import functools

import jax
import jax.numpy as jnp
from jax import lax
from jax.experimental import pallas as pl
from jax.experimental.pallas import tpu as pltpu
from jax.sharding import PartitionSpec as P

MESH = pl.DeviceIdType.MESH
F32 = jnp.float32
BF16 = jnp.bfloat16
TAIL = 16
CHUNK = 128
BLOCK = 1024


def split3(value):
    high = value.astype(BF16).astype(F32)
    rest = value - high
    middle = rest.astype(BF16).astype(F32)
    return high, middle, rest - middle


def eye_mask(size):
    down = lax.broadcasted_iota(jnp.int32, (size, size), 0)
    across = lax.broadcasted_iota(jnp.int32, (size, size), 1)
    return down == across


def to_row(column, size):
    spread = jnp.broadcast_to(column, (size, size))
    return jnp.sum(jnp.where(eye_mask(size), spread, 0.0), axis=0, keepdims=True)


def to_column(row, size):
    spread = jnp.broadcast_to(row, (size, size))
    return jnp.sum(jnp.where(eye_mask(size), spread, 0.0), axis=1, keepdims=True)


def kernel(
    regions,
    group,
    owner_ref,
    readers_ref,
    obs_rows_ref,
    x_ref,
    values_ref,
    errors_ref,
    order_ref,
    taper_ref,
    out_ref,
    picked,
    z_out,
    z_in,
    full,
    prior,
    table,
    params,
    anom,
    push,
    z_send,
    z_recv,
    chip_send,
    chip_recv,
    core_send,
    core_recv,
):
    batches, obs = order_ref.shape
    rows, members = x_ref.shape
    slots = obs // group
    chips = group // 2
    steps = regions.bit_length() - 1
    block = min(BLOCK, rows, obs)
    region = lax.axis_index("region")
    me = lax.axis_index("rows")
    chip, core = me // 2, me % 2
    sibling = chip * 2 + 1 - core

    def across(step):
        bit = 2**step
        return region + bit - 2 * bit * ((region // bit) % 2)

    def z_copy(step, b):
        return pltpu.make_async_remote_copy(
            src_ref=z_out.at[step, b],
            dst_ref=z_in.at[step, b],
            send_sem=z_send.at[step, b],
            recv_sem=z_recv.at[step, b],
            device_id=(across(step), me),
            device_id_type=MESH,
        )

    def chip_copy(b, k):
        return pltpu.make_async_remote_copy(
            src_ref=full.at[b, me],
            dst_ref=full.at[b, me],
            send_sem=chip_send.at[b, k],
            recv_sem=chip_recv.at[b, k],
            device_id=(region, ((chip + k) % chips) * 2 + core),
            device_id_type=MESH,
        )

    def core_copy(b, k):
        place = ((chip + chips - k) % chips) * 2 + core
        return pltpu.make_async_remote_copy(
            src_ref=full.at[b, place],
            dst_ref=full.at[b, place],
            send_sem=core_send.at[b, k],
            recv_sem=core_recv.at[b, k],
            device_id=(region, sibling),
            device_id_type=MESH,
        )

    barrier = pltpu.get_barrier_semaphore()
    for step in range(steps):
        pl.semaphore_signal(barrier, inc=1, device_id=(across(step), me), device_id_type=MESH)
    for k in range(1, chips):
        pl.semaphore_signal(
            barrier, inc=1, device_id=(region, ((chip + k) % chips) * 2 + core), device_id_type=MESH
        )
    pl.semaphore_signal(barrier, inc=1, device_id=(region, sibling), device_id_type=MESH)

    def pick(b):
        def eight(i, carry):
            base = pl.multiple_of(i * 8, 8)
            for r in range(8):
                index = obs_rows_ref[b, me * slots + base + r]
                picked[pl.ds(base + r, 1), :] = x_ref[pl.ds(index, 1), :]
            return carry

        lax.fori_loop(0, slots // 8, eight, 0, unroll=2)
        mine = jnp.where(owner_ref[b] == region, 1.0, 0.0).astype(F32)
        held = picked[...]
        mean = jnp.mean(held, axis=1, keepdims=True)
        z_out[0, b, pl.ds(0, slots), :] = ((held - mean) * mine).astype(BF16)
        parts = split3(to_row(mean * mine, slots))
        index = lax.broadcasted_iota(jnp.int32, (TAIL, slots), 0)
        tail = jnp.zeros((TAIL, slots), F32)
        for n, part in enumerate(parts):
            tail = jnp.where(index == n, jnp.broadcast_to(part, (TAIL, slots)), tail)
        z_out[0, b, pl.ds(slots, TAIL), :] = jnp.concatenate(
            [tail, jnp.zeros((TAIL, members - slots), F32)], axis=1
        ).astype(BF16)

    def reads(b, target):
        found = owner_ref[b] == target
        for n in range(readers_ref.shape[1]):
            found = jnp.logical_or(found, readers_ref[b, n] == target)
        return jnp.where(found, 1.0, 0.0).astype(F32)

    def permute(b):
        table[0:1, :] = values_ref[b : b + 1, :]
        table[1:2, :] = errors_ref[b : b + 1, :]
        for v in range(batches):
            if v == 0:
                target = region
            elif v > b:
                target = owner_ref[v]
            else:
                continue
            table[2 + v : 3 + v, :] = taper_ref[b, pl.ds(target, 1), :] * reads(b, target)
        high, middle, low = split3(table[...])
        stacked = jnp.concatenate([high, middle, low, jnp.zeros_like(low)], axis=0).astype(BF16)
        lane = lax.broadcasted_iota(jnp.int32, (CHUNK, obs), 1).astype(F32)
        for n in range(obs // CHUNK):
            number = to_column(
                order_ref[b : b + 1, n * CHUNK : (n + 1) * CHUNK].astype(F32), CHUNK
            )
            chosen = jnp.where(number == lane, 1.0, 0.0).astype(BF16)
            got = lax.dot_general(
                chosen, stacked, (((1,), (1,)), ((), ())), preferred_element_type=F32
            )
            params[b, n * CHUNK : (n + 1) * CHUNK, :] = (
                got[:, 0:8] + got[:, 8:16] + got[:, 16:24]
            )

    def spread_out(b):
        last = steps - 1
        z_copy(last, b).wait_recv()
        full[b, me] = z_out[last, b] + z_in[last, b]
        for k in range(1, chips):
            chip_copy(b, k).start()
        core_copy(b, 0).start()

    def hand_over(b):
        for k in range(1, chips):
            chip_copy(b, k).wait_recv()
            core_copy(b, k).start()

    def place(b):
        for k in range(chips):
            core_copy(b, k).wait_recv()

        def one(g, carry):
            tail = full[b, g, pl.ds(slots, TAIL), :][:, :slots].astype(F32)
            mean = to_column(tail[0:1] + tail[1:2] + tail[2:3], slots)
            start = pl.multiple_of(b * obs + g * slots, slots)
            prior[pl.ds(start, slots), :] = full[b, g, pl.ds(0, slots), :].astype(F32) + mean
            return carry

        lax.fori_loop(0, group, one, 0, unroll=4)

    def prepare(b):
        def one(n, carry):
            start = pl.multiple_of(n * CHUNK, CHUNK)
            held = prior[pl.ds(b * obs + start, CHUNK), :]
            param = params[b, pl.ds(start, CHUNK), :]
            value, error = param[:, 0:1], param[:, 1:2]
            mean = jnp.mean(held, axis=1, keepdims=True)
            away = held - mean
            variance = jnp.sum(away * away, axis=1, keepdims=True) / (members - 1) + 1e-05
            total = 1.0 / (variance + error)
            shift = variance * (value - mean) * total
            shrink = jnp.sqrt(error * total)
            increment = shift + (shrink - 1.0) * away
            anom[pl.ds(start, CHUNK), :] = away.astype(BF16)
            inverse = 1.0 / ((members - 1) * variance)
            for v in range(batches):
                if v == 0 or v > b:
                    weight = param[:, 2 + v : 3 + v] * inverse
                    push[v, pl.ds(start, CHUNK), :] = (increment * weight).astype(BF16)
            return carry

        lax.fori_loop(0, obs // CHUNK, one, 0, unroll=4)

    def updated(held, variant):
        mean = jnp.mean(held, axis=1, keepdims=True)
        away = (held - mean).astype(BF16)
        linked = lax.dot_general(
            away, anom[...], (((1,), (1,)), ((), ())), preferred_element_type=F32
        ).astype(BF16)
        return held + jnp.dot(linked, push[variant], preferred_element_type=F32)

    def observed(b, first, last):
        per = obs // block

        def one(i, carry):
            at = pl.ds(pl.multiple_of(i * block, block), block)
            prior[at, :] = updated(prior[at, :], i // per)
            return carry

        lax.fori_loop(first * per, last * per, one, 0)

    def state(b, source, first, last):
        def one(i, carry):
            at = pl.ds(pl.multiple_of(i * wide, wide), wide)
            out_ref[at, :] = updated(source[at, :], 0)
            return carry

        lax.fori_loop(first, last, one, 0)

    pick(0)
    pl.semaphore_wait(barrier, steps + chips)
    z_copy(0, 0).start()
    for b in range(1, batches):
        pick(b)
        z_copy(0, b).start()
    table[...] = jnp.zeros_like(table)
    permute(0)
    for step in range(1, steps):
        for b in range(batches):
            z_copy(step - 1, b).wait_recv()
            z_out[step, b] = z_out[step - 1, b] + z_in[step - 1, b]
            z_copy(step, b).start()
    wide = min(2 * BLOCK, rows)
    blocks = rows // wide
    for b in range(1, batches):
        spread_out(b - 1)
        if b > 1:
            hand_over(b - 2)
        permute(b)
        if b == 2:
            place(0)
            prepare(0)
    spread_out(batches - 1)
    pending = [batches - 2, batches - 1]
    hand_over(pending[0])
    state(0, x_ref, 0, blocks)
    hand_over(pending[1])
    for b in range(1, batches):
        place(b)
        observed(0, b, b + 1)
    for b in range(1, batches):
        prepare(b)
        if b + 1 < batches:
            observed(b, b + 1, batches)
        state(b, out_ref, 0, blocks)
    for b in range(batches):
        for step in range(steps):
            z_copy(step, b).wait_send()
        for k in range(chips):
            if k:
                chip_copy(b, k).wait_send()
            core_copy(b, k).wait_send()


def local(regions, group, state, values, errors, owner, readers, order, obs_rows, taper):
    batches, obs = order.shape
    rows, members = state.shape
    slots = obs // group
    chips = group // 2
    steps = regions.bit_length() - 1
    packet = (slots + TAIL, members)
    smem = pl.BlockSpec(memory_space=pltpu.SMEM)
    vmem = pl.BlockSpec(memory_space=pltpu.VMEM)
    dma = pltpu.SemaphoreType.DMA
    return pl.pallas_call(
        functools.partial(kernel, regions, group),
        out_shape=jax.ShapeDtypeStruct((rows, members), F32),
        in_specs=[smem] * 3 + [vmem] * 5,
        out_specs=vmem,
        scratch_shapes=[
            pltpu.VMEM((slots, members), F32),
            pltpu.VMEM((steps, batches) + packet, BF16),
            pltpu.VMEM((steps, batches) + packet, BF16),
            pltpu.VMEM((batches, group) + packet, BF16),
            pltpu.VMEM((batches * obs, members), F32),
            pltpu.VMEM((8, obs), F32),
            pltpu.VMEM((batches, obs, 8), F32),
            pltpu.VMEM((obs, members), BF16),
            pltpu.VMEM((batches, obs, members), BF16),
            dma((steps, batches)),
            dma((steps, batches)),
            dma((batches, chips)),
            dma((batches, chips)),
            dma((batches, chips)),
            dma((batches, chips)),
        ],
        compiler_params=pltpu.CompilerParams(
            collective_id=0, has_side_effects=True, vmem_limit_bytes=63 * 2**20
        ),
    )(owner, readers, obs_rows, state, values, errors, order, taper)


def solution(mesh):
    placed = (P(("region", "rows"), None), P(), P(), P(), P(), P(), P(), P())
    return jax.shard_map(
        functools.partial(local, mesh.shape["region"], mesh.shape["rows"]),
        mesh=mesh,
        in_specs=placed,
        out_specs=P(("region", "rows"), None),
        check_vma=False,
    )
```

```python
import functools

import jax
import jax.numpy as jnp
from jax import lax
from jax.experimental import pallas as pl
from jax.experimental.pallas import tpu as pltpu
from jax.sharding import PartitionSpec as P

MESH = pl.DeviceIdType.MESH
F32 = jnp.float32
BF16 = jnp.bfloat16
TAIL = 16
CHUNK = 128
BLOCK = 1024


def split3(value):
    high = value.astype(BF16).astype(F32)
    rest = value - high
    middle = rest.astype(BF16).astype(F32)
    return high, middle, rest - middle


def eye_mask(size):
    down = lax.broadcasted_iota(jnp.int32, (size, size), 0)
    across = lax.broadcasted_iota(jnp.int32, (size, size), 1)
    return down == across


def to_row(column, size):
    spread = jnp.broadcast_to(column, (size, size))
    return jnp.sum(jnp.where(eye_mask(size), spread, 0.0), axis=0, keepdims=True)


def to_column(row, size):
    spread = jnp.broadcast_to(row, (size, size))
    return jnp.sum(jnp.where(eye_mask(size), spread, 0.0), axis=1, keepdims=True)


def kernel(
    regions,
    group,
    owner_ref,
    readers_ref,
    obs_rows_ref,
    x_ref,
    values_ref,
    errors_ref,
    order_ref,
    taper_ref,
    out_ref,
    picked,
    z_out,
    z_in,
    full,
    prior,
    table,
    params,
    anom,
    push,
    z_send,
    z_recv,
    chip_send,
    chip_recv,
    core_send,
    core_recv,
    half_send,
    half_recv,
):
    batches, obs = order_ref.shape
    rows, members = x_ref.shape
    slots = obs // group
    chips = group // 2
    steps = regions.bit_length() - 1
    half = obs // 2
    region = lax.axis_index("region")
    me = lax.axis_index("rows")
    chip, core = me // 2, me % 2
    sibling = chip * 2 + 1 - core

    def across(step):
        bit = 2**step
        return region + bit - 2 * bit * ((region // bit) % 2)

    def z_copy(step, b):
        return pltpu.make_async_remote_copy(
            src_ref=z_out.at[step, b],
            dst_ref=z_in.at[step, b],
            send_sem=z_send.at[step, b],
            recv_sem=z_recv.at[step, b],
            device_id=(across(step), me),
            device_id_type=MESH,
        )

    def chip_copy(b, k):
        return pltpu.make_async_remote_copy(
            src_ref=full.at[b, me],
            dst_ref=full.at[b, me],
            send_sem=chip_send.at[b, k],
            recv_sem=chip_recv.at[b, k],
            device_id=(region, ((chip + k) % chips) * 2 + core),
            device_id_type=MESH,
        )

    def core_copy(b, k):
        place = ((chip + chips - k) % chips) * 2 + core
        return pltpu.make_async_remote_copy(
            src_ref=full.at[b, place],
            dst_ref=full.at[b, place],
            send_sem=core_send.at[b, k],
            recv_sem=core_recv.at[b, k],
            device_id=(region, sibling),
            device_id_type=MESH,
        )

    def half_copy(b):
        part = prior.at[pl.ds(pl.multiple_of(b * obs + core * half, half), half)]
        return pltpu.make_async_remote_copy(
            src_ref=part,
            dst_ref=part,
            send_sem=half_send.at[b],
            recv_sem=half_recv.at[b],
            device_id=(region, sibling),
            device_id_type=MESH,
        )

    barrier = pltpu.get_barrier_semaphore()
    for step in range(steps):
        pl.semaphore_signal(barrier, inc=1, device_id=(across(step), me), device_id_type=MESH)
    for k in range(1, chips):
        pl.semaphore_signal(
            barrier, inc=1, device_id=(region, ((chip + k) % chips) * 2 + core), device_id_type=MESH
        )
    pl.semaphore_signal(barrier, inc=1, device_id=(region, sibling), device_id_type=MESH)

    def pick(b):
        def eight(i, carry):
            base = pl.multiple_of(i * 8, 8)
            for r in range(8):
                index = obs_rows_ref[b, me * slots + base + r]
                picked[pl.ds(base + r, 1), :] = x_ref[pl.ds(index, 1), :]
            return carry

        lax.fori_loop(0, slots // 8, eight, 0, unroll=2)
        mine = jnp.where(owner_ref[b] == region, 1.0, 0.0).astype(F32)
        held = picked[...]
        mean = jnp.mean(held, axis=1, keepdims=True)
        z_out[0, b, pl.ds(0, slots), :] = ((held - mean) * mine).astype(BF16)
        parts = split3(to_row(mean * mine, slots))
        index = lax.broadcasted_iota(jnp.int32, (TAIL, slots), 0)
        tail = jnp.zeros((TAIL, slots), F32)
        for n, part in enumerate(parts):
            tail = jnp.where(index == n, jnp.broadcast_to(part, (TAIL, slots)), tail)
        z_out[0, b, pl.ds(slots, TAIL), :] = jnp.concatenate(
            [tail, jnp.zeros((TAIL, members - slots), F32)], axis=1
        ).astype(BF16)

    def reads(b, target):
        found = owner_ref[b] == target
        for n in range(readers_ref.shape[1]):
            found = jnp.logical_or(found, readers_ref[b, n] == target)
        return jnp.where(found, 1.0, 0.0).astype(F32)

    def permute(b):
        table[0:1, :] = values_ref[b : b + 1, :]
        table[1:2, :] = errors_ref[b : b + 1, :]
        for v in range(batches):
            if v == 0:
                target = region
            elif v > b:
                target = owner_ref[v]
            else:
                continue
            table[2 + v : 3 + v, :] = taper_ref[b, pl.ds(target, 1), :] * reads(b, target)
        high, middle, low = split3(table[...])
        stacked = jnp.concatenate([high, middle, low, jnp.zeros_like(low)], axis=0).astype(BF16)
        lane = lax.broadcasted_iota(jnp.int32, (CHUNK, obs), 1).astype(F32)
        for n in range(obs // CHUNK):
            number = to_column(
                order_ref[b : b + 1, n * CHUNK : (n + 1) * CHUNK].astype(F32), CHUNK
            )
            chosen = jnp.where(number == lane, 1.0, 0.0).astype(BF16)
            got = lax.dot_general(
                chosen, stacked, (((1,), (1,)), ((), ())), preferred_element_type=F32
            )
            params[b, n * CHUNK : (n + 1) * CHUNK, :] = (
                got[:, 0:8] + got[:, 8:16] + got[:, 16:24]
            )

    def spread_out(b):
        last = steps - 1
        z_copy(last, b).wait_recv()
        full[b, me] = z_out[last, b] + z_in[last, b]
        for k in range(1, chips):
            chip_copy(b, k).start()
        core_copy(b, 0).start()

    def hand_over(b):
        for k in range(1, chips):
            chip_copy(b, k).wait_recv()
            core_copy(b, k).start()

    def place(b):
        for k in range(chips):
            core_copy(b, k).wait_recv()

        def one(g, carry):
            tail = full[b, g, pl.ds(slots, TAIL), :][:, :slots].astype(F32)
            mean = to_column(tail[0:1] + tail[1:2] + tail[2:3], slots)
            start = pl.multiple_of(b * obs + g * slots, slots)
            prior[pl.ds(start, slots), :] = full[b, g, pl.ds(0, slots), :].astype(F32) + mean
            return carry

        if b == 0:
            lax.fori_loop(0, group, one, 0, unroll=4)
        else:
            lax.fori_loop(
                0, chips, lambda n, carry: one(core * chips + n, carry), 0, unroll=4
            )

    def prepare(b):
        def one(n, carry):
            start = pl.multiple_of(n * CHUNK, CHUNK)
            held = prior[pl.ds(b * obs + start, CHUNK), :]
            param = params[b, pl.ds(start, CHUNK), :]
            value, error = param[:, 0:1], param[:, 1:2]
            mean = jnp.mean(held, axis=1, keepdims=True)
            away = held - mean
            variance = jnp.sum(away * away, axis=1, keepdims=True) / (members - 1) + 1e-05
            total = 1.0 / (variance + error)
            shift = variance * (value - mean) * total
            shrink = jnp.sqrt(error * total)
            increment = shift + (shrink - 1.0) * away
            anom[pl.ds(start, CHUNK), :] = away.astype(BF16)
            inverse = 1.0 / ((members - 1) * variance)
            for v in range(batches):
                if v == 0 or v > b:
                    weight = param[:, 2 + v : 3 + v] * inverse
                    push[v, pl.ds(start, CHUNK), :] = (increment * weight).astype(BF16)
            return carry

        lax.fori_loop(0, obs // CHUNK, one, 0, unroll=4)

    def updated(held, variant):
        mean = jnp.mean(held, axis=1, keepdims=True)
        away = (held - mean).astype(BF16)
        linked = lax.dot_general(
            away, anom[...], (((1,), (1,)), ((), ())), preferred_element_type=F32
        ).astype(BF16)
        return held + jnp.dot(linked, push[variant], preferred_element_type=F32)

    def observed(b, first, last):
        for c in range(first, last):
            at = pl.ds(pl.multiple_of(c * obs + core * half, half), half)
            prior[at, :] = updated(prior[at, :], c)
            if c == b + 1:
                half_copy(c).start()

    def state(b, source, first, last):
        def one(i, carry):
            at = pl.ds(pl.multiple_of(i * wide, wide), wide)
            out_ref[at, :] = updated(source[at, :], 0)
            return carry

        lax.fori_loop(first, last, one, 0)

    pick(0)
    pl.semaphore_wait(barrier, steps + chips)
    z_copy(0, 0).start()
    for b in range(1, batches):
        pick(b)
        z_copy(0, b).start()
    table[...] = jnp.zeros_like(table)
    permute(0)
    for step in range(1, steps):
        for b in range(batches):
            z_copy(step - 1, b).wait_recv()
            z_out[step, b] = z_out[step - 1, b] + z_in[step - 1, b]
            z_copy(step, b).start()
    wide = min(2 * BLOCK, rows)
    blocks = rows // wide
    for b in range(1, batches):
        spread_out(b - 1)
        if b > 1:
            hand_over(b - 2)
        permute(b)
        if b == 2:
            place(0)
            prepare(0)
    spread_out(batches - 1)
    pending = [batches - 2, batches - 1]
    hand_over(pending[0])
    state(0, x_ref, 0, blocks)
    hand_over(pending[1])
    for b in range(1, batches):
        place(b)
        observed(0, b, b + 1)
    for b in range(1, batches):
        half_copy(b).wait_recv()
        prepare(b)
        observed(b, b + 1, batches)
        state(b, out_ref, 0, blocks)
    for b in range(batches):
        for step in range(steps):
            z_copy(step, b).wait_send()
        for k in range(chips):
            if k:
                chip_copy(b, k).wait_send()
            core_copy(b, k).wait_send()
        if b:
            half_copy(b).wait_send()


def local(regions, group, state, values, errors, owner, readers, order, obs_rows, taper):
    batches, obs = order.shape
    rows, members = state.shape
    slots = obs // group
    chips = group // 2
    steps = regions.bit_length() - 1
    packet = (slots + TAIL, members)
    smem = pl.BlockSpec(memory_space=pltpu.SMEM)
    vmem = pl.BlockSpec(memory_space=pltpu.VMEM)
    dma = pltpu.SemaphoreType.DMA
    return pl.pallas_call(
        functools.partial(kernel, regions, group),
        out_shape=jax.ShapeDtypeStruct((rows, members), F32),
        in_specs=[smem] * 3 + [vmem] * 5,
        out_specs=vmem,
        scratch_shapes=[
            pltpu.VMEM((slots, members), F32),
            pltpu.VMEM((steps, batches) + packet, BF16),
            pltpu.VMEM((steps, batches) + packet, BF16),
            pltpu.VMEM((batches, group) + packet, BF16),
            pltpu.VMEM((batches * obs, members), F32),
            pltpu.VMEM((8, obs), F32),
            pltpu.VMEM((batches, obs, 8), F32),
            pltpu.VMEM((obs, members), BF16),
            pltpu.VMEM((batches, obs, members), BF16),
            dma((steps, batches)),
            dma((steps, batches)),
            dma((batches, chips)),
            dma((batches, chips)),
            dma((batches, chips)),
            dma((batches, chips)),
            dma((batches,)),
            dma((batches,)),
        ],
        compiler_params=pltpu.CompilerParams(
            collective_id=0, has_side_effects=True, vmem_limit_bytes=63 * 2**20
        ),
    )(owner, readers, obs_rows, state, values, errors, order, taper)


def solution(mesh):
    placed = (P(("region", "rows"), None), P(), P(), P(), P(), P(), P(), P())
    return jax.shard_map(
        functools.partial(local, mesh.shape["region"], mesh.shape["rows"]),
        mesh=mesh,
        in_specs=placed,
        out_specs=P(("region", "rows"), None),
        check_vma=False,
    )
```
